32 devices in a mesh: row: 16 (over z, x, core), col: 2 (over y).
Axes of the slice: x: 2, y: 2, z: 4, core: 2. Of those that a mesh axis runs over, the one named last changes fastest.
Arguments:
- density: bfloat16 [6144, 6144], P('col', 'row'), may hold values from -1.5 to 1.5
- block_mask: int32 [48, 48], replicated, may hold values from 0 to 1, as said below
- owner: int32 [4, 2], replicated, may hold values from 0 to 15, as said below
Outputs:
- square_part: float32 [6144, 6144], P('col', 'row')
The draws below stay inside these ranges and needn't reach their ends.
Inputs may be any that keep to these rules, and one draw needn't show every extreme that they name: owner[t, g] // 8 equals (g + t) mod 2. `block_mask`: each tile of 24 x 3 blocks (block rows g * 24 onward, block columns j * 3 onward) has at most 43 entries equal to 1, and in every draw some tile has exactly 43.
All inputs are finite; a program needn't handle non-finite values.
Results may differ from the reference program's by a relative error of at most 0.0003.
Values may be sent and summed in bfloat16 or wider, within the bound.
No kernel may reach another device: no remote copies, remote signals or barrier semaphores. Data moves between devices by JAX's collectives and lax.ppermute only.
A program may use at most 64 MiB of HBM per device.

```python
import jax
import jax.numpy as jnp
from jax import lax

BLOCK = 128
TC = 3
STEPS = 4
SUB = 8
TR = 24
CAP = 43
ORDER = 6144
N_ROW = 16
N_COL = 2


def draw_block_mask(key, part):
    key = jax.random.fold_in(key, 11)
    tiles = N_COL * N_ROW
    cells = TR * TC
    key_count, key_full, key_place = jax.random.split(key, 3)
    halvings = jax.random.randint(key_count, (tiles,), 0, 4)
    counts = CAP // jnp.left_shift(jnp.ones((tiles,), jnp.int32), halvings)
    fullest = jax.random.randint(key_full, (), 0, tiles)
    counts = jnp.where(jnp.arange(tiles) == fullest, CAP, counts)
    scores = jax.random.randint(key_place, (tiles, cells), 0, 1 << 20) * cells + jnp.arange(cells)[None, :]
    ranks = jnp.argsort(jnp.argsort(scores, axis=1), axis=1)
    flags = (ranks < counts[:, None]).astype(jnp.int32)
    flags = flags.reshape(N_COL, N_ROW, TR, TC).transpose(0, 2, 1, 3)
    return flags.reshape(N_COL * TR, N_ROW * TC)


def draw_owner(key, part):
    key = jax.random.fold_in(key, 23)
    sections = jnp.arange(STEPS, dtype=jnp.int32)[:, None]
    grid_rows = jnp.arange(N_COL, dtype=jnp.int32)[None, :]
    picks = jax.random.randint(key, (STEPS, N_COL), 0, SUB)
    first_section = sections == 0
    picks = jnp.where(first_section & (grid_rows == 0), 0, picks)
    picks = jnp.where(first_section & (grid_rows == N_COL - 1), SUB - 1, picks)
    return (SUB * ((grid_rows + sections) % N_COL) + picks).astype(jnp.int32)


def block_levels(stream_key, dims, shards, least, largest):
    def one(position, shards_of):
        heights = jax.random.uniform(jax.random.fold_in(jax.random.fold_in(stream_key, 6), position), (shards_of,), jnp.float32, least / len(shards), largest / len(shards))
        return jnp.repeat(jnp.exp(heights), dims[position] // shards_of).reshape((-1,) + (1,) * (len(dims) - position - 1))

    level = one(*shards[0])
    for cut in shards[1:]:
        level = level * one(*cut)
    return level


def normal_values(rng, shape, spread, reach, cuts=(), kind=jnp.bfloat16):
    loudness = block_levels(rng, shape, cuts, -0.22, 0.18) if cuts else 1.0
    array = jax.random.normal(rng, shape, jnp.float32) * spread * loudness
    return jnp.minimum(jnp.maximum(array, -reach), reach).astype(kind)


def setup_inputs(seed: int = 0) -> dict:
    streams_of = jax.random.split(jax.random.key(seed), 4)
    density = normal_values(streams_of[0], (ORDER, ORDER), 0.25, 1.5, ((0, 2), (1, 16)))
    block_mask = draw_block_mask(jax.random.fold_in(streams_of[3], 71), 0)
    owner = draw_owner(jax.random.fold_in(streams_of[3], 71), 0)
    return {"density": density, "block_mask": block_mask, "owner": owner}


def masked_matrix(density, block_mask):
    blocks_down = block_mask.shape[0]
    blocks_across = block_mask.shape[1]
    shaped = density.reshape(blocks_down, BLOCK, blocks_across, BLOCK)
    kept = jnp.where(block_mask[:, None, :, None] == 1, shaped, jnp.zeros((), jnp.bfloat16))
    return kept.reshape(density.shape)


def reference(density, block_mask, owner):
    masked = masked_matrix(density, block_mask)
    slab_rows = ORDER // N_COL
    slab_width = TC * BLOCK

    def one_slab(grid_row):
        offset_rows = (grid_row * slab_rows).astype(jnp.int32)
        rows_here = lax.dynamic_slice_in_dim(masked, offset_rows, slab_rows, 0)
        accumulated = jnp.zeros((slab_rows, ORDER), jnp.float32)
        for section_index in range(STEPS):
            offset = (owner[section_index, grid_row] * slab_width).astype(jnp.int32)
            left_tile = lax.dynamic_slice_in_dim(rows_here, offset, slab_width, 1)
            right_rows = lax.dynamic_slice_in_dim(masked, offset, slab_width, 0)
            accumulated = accumulated + jnp.dot(left_tile, right_rows, preferred_element_type=jnp.float32)
        return accumulated

    all_slabs = lax.map(one_slab, jnp.arange(N_COL, dtype=jnp.int32))
    return all_slabs.reshape(ORDER, ORDER)
```

```python
import functools

import jax
import jax.numpy as jnp
from jax import lax
from jax.experimental import pallas as pl
from jax.experimental.pallas import tpu as pltpu
from jax.sharding import PartitionSpec as P

BLOCK = 128
STEPS = 4
GROUPS = 4
RUN_BITS = 2
RUN = 1 << RUN_BITS
LIST = 128

VMEM = pl.BlockSpec(memory_space=pltpu.VMEM)
SMEM = pl.BlockSpec(memory_space=pltpu.SMEM)
ANY = pl.BlockSpec(memory_space=pl.ANY)
SMALL = pl.CostEstimate(flops=1000, bytes_accessed=1000, transcendentals=0)
LARGE = pl.CostEstimate(flops=10**10, bytes_accessed=40 * 2**20, transcendentals=0)


class Plan:
    def __init__(self, row_count, col_count, tile_rows, tile_width):
        self.row_count = row_count
        self.col_count = col_count
        self.tile_rows = tile_rows
        self.tile_width = tile_width
        self.row_blocks = tile_rows // BLOCK
        self.col_blocks = tile_width // BLOCK
        self.cells = self.row_blocks * self.col_blocks
        self.group = row_count // col_count
        self.cap = self.cells * 3 // 5
        self.piece = BLOCK // self.group
        self.held = max(1, STEPS // col_count)
        self.shifts = [
            [t for t in range(STEPS) if t % col_count == s]
            for s in range(min(col_count, STEPS))
        ]


def list_blocks(plan, mask, row0, col0, put, marks):
    together = 4

    def some_rows(m, count):
        cells = [(m * together + i, c) for i in range(together) for c in range(plan.col_blocks)]
        kept = [mask[row0 + r, col0 + c] for r, c in cells]
        for (r, c), one in zip(cells, kept):
            put(count, r, c)
            count = count + one
        return count

    counts = [jnp.int32(0)]
    for first, last in zip(marks[:-1], marks[1:]):
        counts.append(
            lax.fori_loop(first // together, last // together, some_rows, counts[-1])
        )
    return counts


def pack_kernel(plan, mask_any, tile_any, *refs):
    *outs, tile, mask, listed, tile_sems, mask_sem = refs
    grid_col = lax.axis_index("row")
    row0 = lax.axis_index("col") * plan.row_blocks
    col0 = grid_col * plan.col_blocks
    chunks = 6
    chunk_blocks = plan.row_blocks // chunks
    marks = [q * chunk_blocks for q in range(chunks + 1)]

    mask_copy = pltpu.make_async_copy(mask_any, mask, mask_sem)
    mask_copy.start()
    copies = []
    for q in range(chunks):
        rows = pl.ds(marks[q] * plan.group, chunk_blocks * plan.group)
        copy = pltpu.make_async_copy(tile_any.at[rows], tile.at[rows], tile_sems.at[q])
        copy.start()
        copies.append(copy)
    mask_copy.wait()

    def put(n, r, c):
        listed[n] = 4 * r + c

    counts = list_blocks(plan, mask, row0, col0, put, marks)
    place = lax.rem(grid_col, plan.group)
    parts = [jnp.bitwise_xor(place, k) for k in range(plan.group)]

    def one_block(n, carry):
        code = listed[n]
        top = lax.shift_right_logical(code, 2) * plan.group
        left = pl.multiple_of(jnp.bitwise_and(code, 3) * BLOCK, BLOCK)
        for k in range(plan.group):
            block = tile[top + parts[k], :, pl.ds(left, BLOCK)]
            outs[k % len(outs)][k // len(outs), n] = block
        return carry

    for q in range(chunks):
        copies[q].wait()
        lax.fori_loop(counts[q], counts[q + 1], one_block, 0)


def pack(plan, count, mask, tile):
    pieces = (plan.group // count, plan.cap, plan.piece, BLOCK)
    tile = tile.reshape(-1, plan.piece, plan.tile_width)
    return pl.pallas_call(
        functools.partial(pack_kernel, plan),
        out_shape=[jax.ShapeDtypeStruct(pieces, jnp.bfloat16)] * count,
        in_specs=[ANY, ANY],
        out_specs=[VMEM] * count,
        scratch_shapes=[
            pltpu.VMEM(tile.shape, jnp.bfloat16),
            pltpu.SMEM(mask.shape, jnp.int32),
            pltpu.SMEM((plan.cells,), jnp.int32),
            pltpu.SemaphoreType.DMA((6,)),
            pltpu.SemaphoreType.DMA,
        ],
        compiler_params=pltpu.CompilerParams(vmem_limit_bytes=60 * 2**20),
        name="pack",
    )(mask, tile)


def slabs_kernel(plan, mask, owner, tile, *refs):
    slabs = refs[: len(plan.shifts)]
    found, sems = refs[len(plan.shifts) :]
    grid_row = lax.axis_index("col")
    row0 = grid_row * plan.row_blocks
    col0 = lax.axis_index("row") * plan.col_blocks
    width = plan.tile_width
    wanted = []
    for s, steps in enumerate(plan.shifts):
        target = lax.rem(grid_row - s + plan.col_count, plan.col_count)
        for i, t in enumerate(steps):
            first = lax.rem(owner[target, t], plan.group)
            copy = pltpu.make_async_copy(
                tile.at[pl.ds(pl.multiple_of(first * width, width), width)],
                found.at[t],
                sems.at[t],
            )
            copy.start()
            wanted.append((s, i, t, first * plan.col_blocks, copy))
    for s, i, t, first, copy in wanted:
        copy.wait()
        for r in range(plan.col_blocks):
            for c in range(plan.col_blocks):
                kept = mask[row0 + first + r, col0 + c]
                block = found[t, r * BLOCK : (r + 1) * BLOCK, c * BLOCK : (c + 1) * BLOCK]
                to = i * width + r * BLOCK
                slabs[s][to : to + BLOCK, c * BLOCK : (c + 1) * BLOCK] = jnp.where(
                    kept == 1, block, jnp.zeros_like(block)
                )


def slabs_of(plan, mask, owner, tile):
    width = plan.tile_width
    return pl.pallas_call(
        functools.partial(slabs_kernel, plan),
        out_shape=[
            jax.ShapeDtypeStruct((len(s) * width, width), jnp.bfloat16) for s in plan.shifts
        ],
        in_specs=[SMEM, SMEM, ANY],
        out_specs=[VMEM] * len(plan.shifts),
        scratch_shapes=[
            pltpu.VMEM((STEPS, width, width), jnp.bfloat16),
            pltpu.SemaphoreType.DMA((STEPS,)),
        ],
        cost_estimate=SMALL,
        compiler_params=pltpu.CompilerParams(vmem_limit_bytes=8 * 2**20),
        name="slabs",
    )(mask, owner, tile)


def lists_kernel(plan, mask, owner, lists):
    grid_row = lax.axis_index("col")
    row0 = grid_row * plan.row_blocks
    for t in range(STEPS):

        def put(n, r, c):
            lists[t, n] = c * GROUPS * plan.row_blocks + r

        col0 = owner[grid_row, t] * plan.col_blocks
        count = list_blocks(plan, mask, row0, col0, put, [0, plan.row_blocks])[-1]
        lists[t, LIST - 1] = count


def lists_of(plan, mask, owner):
    return pl.pallas_call(
        functools.partial(lists_kernel, plan),
        out_shape=jax.ShapeDtypeStruct((STEPS, LIST), jnp.int32),
        in_specs=[SMEM, SMEM],
        out_specs=SMEM,
        cost_estimate=SMALL,
        compiler_params=pltpu.CompilerParams(vmem_limit_bytes=2 * 2**20),
        name="lists",
    )(mask, owner)


def counts_kernel(plan, branches, mask, owner, counts):
    grid_row = lax.axis_index("col")
    most = jnp.int32(0)
    chip_most = jnp.int32(0)
    for g in range(plan.col_count):
        kept = mask[g * plan.row_blocks : (g + 1) * plan.row_blocks, :]
        column = lax.broadcasted_iota(jnp.int32, kept.shape, 1)
        found = []
        for t in range(STEPS):
            col0 = owner[g, t] * plan.col_blocks
            inside = (column >= col0) & (column < col0 + plan.col_blocks)
            found.append(jnp.sum(jnp.where(inside, kept, 0)))

        @pl.when(grid_row == g)
        def _():
            for t in range(STEPS):
                counts[t] = found[t]

        for t in range(STEPS // 2):
            total = found[t] + found[t + 2]
            one_chip = jnp.bitwise_xor(owner[g, t], owner[g, t + 2]) == 1
            most = jnp.maximum(most, total)
            chip_most = jnp.maximum(chip_most, jnp.where(one_chip, total, 0))
    choice = jnp.int32(len(branches) - 1)
    for i, (capacity, chip_capacity) in reversed(list(enumerate(branches))):
        choice = jnp.where((most <= capacity) & (chip_most <= chip_capacity), i, choice)
    counts[STEPS] = choice


def counts_of(plan, branches, mask, owner):
    return pl.pallas_call(
        functools.partial(counts_kernel, plan, branches),
        out_shape=jax.ShapeDtypeStruct((STEPS + 1,), jnp.int32),
        in_specs=[VMEM, SMEM],
        out_specs=SMEM,
        cost_estimate=SMALL,
        compiler_params=pltpu.CompilerParams(vmem_limit_bytes=2 * 2**20),
        name="counts",
    )(mask, owner)


def copy_blocks(count, copy):
    def run(m, carry):
        for n in range(RUN):
            copy(jnp.minimum(m * RUN + n, count - 1))
        return carry

    lax.fori_loop(0, lax.shift_right_logical(count + RUN - 1, RUN_BITS), run, 0)


def used_tiles(plan, counts, owner):
    grid_row = lax.axis_index("col")
    grid_col = lax.axis_index("row")
    first = lax.rem(lax.div(grid_col, plan.group) + grid_row, 2)
    roots = [lax.rem(owner[grid_row, first + 2 * i], plan.group) for i in range(2)]
    blocks = [counts[first + 2 * i] for i in range(2)]
    return lax.rem(grid_col, plan.group), roots, blocks


def merge_kernel(plan, counts, owner, own, other, *refs):
    *outs, joint = refs
    place, roots, blocks = used_tiles(plan, counts, owner)
    core = jnp.bitwise_and(place, 1)
    lower = place - core
    at = jnp.int32(0)
    for i in range(2):
        count = jnp.where(
            roots[0] == lower + i, blocks[0], jnp.where(roots[1] == lower + i, blocks[1], 0)
        )
        for source, mine in ((own, core == i), (other, core != i)):

            def copy(n, source=source, at=at):
                for d in range(len(outs)):
                    joint[d, at + n] = source[d, n]

            copy_blocks(jnp.where(mine, count, 0), copy)
        at = at + count

    def some(n, carry):
        for d, out in enumerate(outs):
            out[n] = joint[d, n]
        return carry

    lax.fori_loop(0, outs[0].shape[0], some, 0)


def merge(plan, capacity, counts, owner, own, other):
    count = plan.group // 2
    shape = jax.ShapeDtypeStruct((capacity, plan.piece, BLOCK), jnp.bfloat16)
    return pl.pallas_call(
        functools.partial(merge_kernel, plan),
        out_shape=[shape] * count,
        in_specs=[SMEM, SMEM, VMEM, VMEM],
        out_specs=[VMEM] * count,
        scratch_shapes=[pltpu.VMEM((count, 2 * plan.cap, plan.piece, BLOCK), jnp.bfloat16)],
        compiler_params=pltpu.CompilerParams(vmem_limit_bytes=10 * 2**20),
        name="merge",
    )(counts, owner, own, other)


def take_kernel(plan, counts, owner, *refs):
    chips, outs, joint = refs[:-3], refs[-3:-1], refs[-1]
    place, roots, blocks = used_tiles(plan, counts, owner)
    at = jnp.int32(0)
    for i in range(2):
        root, other = roots[i], roots[1 - i]
        behind = (jnp.bitwise_and(root, 1) == 1) & (other == root - 1)
        start = jnp.where(behind, blocks[1 - i], 0)
        distance = lax.shift_right_logical(jnp.bitwise_xor(root, place), 1)
        for d, chip in enumerate(chips):

            def copy(n, chip=chip, at=at):
                joint[at + n] = chip[start + n]

            copy_blocks(jnp.where(distance == d, blocks[i], 0), copy)
        at = at + blocks[i]
    for out in outs:

        def some(m, carry, out=out):
            out[pl.ds(2 * m, 2)] = joint[pl.ds(2 * m, 2)]
            return carry

        lax.fori_loop(0, out.shape[0] // 2, some, 0)


def take(plan, sizes, counts, owner, chips):
    return pl.pallas_call(
        functools.partial(take_kernel, plan),
        out_shape=[
            jax.ShapeDtypeStruct((size, plan.piece, BLOCK), jnp.bfloat16) for size in sizes
        ],
        in_specs=[SMEM, SMEM] + [VMEM] * len(chips),
        out_specs=[VMEM] * len(sizes),
        scratch_shapes=[pltpu.VMEM((2 * plan.cap, plan.piece, BLOCK), jnp.bfloat16)],
        compiler_params=pltpu.CompilerParams(vmem_limit_bytes=8 * 2**20),
        name="take",
    )(counts, owner, *chips)


def pick_kernel(plan, lists, owner, *refs):
    pieces = refs[: plan.group]
    joint = refs[-1]
    outs = refs[plan.group : -1]
    grid_row = lax.axis_index("col")
    grid_col = lax.axis_index("row")
    mine = lax.div(grid_col, plan.group)
    place = lax.rem(grid_col, plan.group)
    first = lax.rem(mine - grid_row + plan.col_count, plan.col_count)
    at = jnp.int32(0)
    for i in range(plan.held):
        step = lax.rem(first + i * plan.col_count, STEPS)
        root = lax.rem(owner[grid_row, step], plan.group)
        for k, piece in enumerate(pieces):

            @pl.when(root == jnp.bitwise_xor(place, k))
            def _():
                joint[pl.ds(at, plan.cap)] = piece[0]

        at = at + lists[step, LIST - 1]
    low = 0
    for out in outs:
        out[...] = joint[low : low + out.shape[0]]
        low += out.shape[0]


def pick(plan, sizes, lists, owner, pieces):
    return pl.pallas_call(
        functools.partial(pick_kernel, plan),
        out_shape=[
            jax.ShapeDtypeStruct((size, plan.piece, BLOCK), jnp.bfloat16) for size in sizes
        ],
        in_specs=[SMEM, SMEM] + [VMEM] * plan.group,
        out_specs=[VMEM] * len(sizes),
        scratch_shapes=[
            pltpu.VMEM((plan.held * plan.cap, plan.piece, BLOCK), jnp.bfloat16),
        ],
        compiler_params=pltpu.CompilerParams(vmem_limit_bytes=8 * 2**20),
        name="pick",
    )(lists, owner, *pieces)


def stack_kernel(ranges, *refs):
    to = 0
    for ref, (low, count) in zip(refs, ranges):
        together = 2 if count % 2 == 0 else 1

        def some(m, carry, ref=ref, low=low, to=to, together=together):
            refs[-1][pl.ds(to + m * together, together)] = ref[
                pl.ds(low + m * together, together)
            ]
            return carry

        lax.fori_loop(0, count // together, some, 0)
        to += count


def stacked(*pieces):
    ranges = [(low, count) for _, low, count in pieces]
    rows = sum(count for _, count in ranges)
    first = pieces[0][0]
    return pl.pallas_call(
        functools.partial(stack_kernel, ranges),
        out_shape=jax.ShapeDtypeStruct((rows,) + first.shape[1:], first.dtype),
        in_specs=[VMEM] * len(pieces),
        out_specs=VMEM,
        cost_estimate=SMALL,
        compiler_params=pltpu.CompilerParams(vmem_limit_bytes=6 * 2**20),
        name="stacked",
    )(*[array for array, _, _ in pieces])


def blank(plan):
    together = 2 * plan.row_blocks

    def body(out):
        def some(m, carry):
            out[pl.ds(m * together, together)] = jnp.zeros((together,) + out.shape[1:], out.dtype)
            return carry

        lax.fori_loop(0, out.shape[0] // together, some, 0)

    parts = STEPS * plan.col_blocks * GROUPS * plan.row_blocks
    return pl.pallas_call(
        body,
        out_shape=jax.ShapeDtypeStruct((parts, plan.piece, BLOCK), jnp.bfloat16),
        out_specs=VMEM,
        cost_estimate=SMALL,
        compiler_params=pltpu.CompilerParams(vmem_limit_bytes=8 * 2**20),
        name="blank",
    )()


def part_kernel(plan, cut, places, lists_any, *refs):
    count = 1 + max(array for _, _, sources in places for both in sources for array, _ in both)
    arrays = refs[:count]
    slabs = refs[count]
    out, left, result, lists, sems, lists_sem = refs[-6:]
    grid_row = lax.axis_index("col")
    grid_col = lax.axis_index("row")
    width = plan.tile_width
    size = plan.piece
    stride = GROUPS * plan.row_blocks
    lists_copy = pltpu.make_async_copy(lists_any, lists, lists_sem)
    lists_copy.start()
    lists_copy.wait()
    for hop in sorted({place[1] for place in places}):
        chosen = range(len(places))
        level = jnp.bitwise_xor(lax.shift_right_logical(grid_col, 2), hop)
        for q in range(2):
            half = lax.shift_right_logical(jnp.bitwise_xor(level, 2 * q), 1)
            first = jnp.bitwise_xor(half, grid_row)
            joint = jnp.int32(0)
            for s in range(plan.held):
                step = first + 2 * s
                origin = (first * plan.held + s) * plan.col_blocks * stride
                blocks = lists[step, LIST - 1]
                split = jnp.minimum(blocks, jnp.maximum(cut - joint, 0))

                def run(m, carry, part, begin, end, shift):
                    for n in range(RUN):
                        n = jnp.minimum(begin + m * RUN + n, end - 1)
                        to = origin + lists[step, n]
                        for i in chosen:
                            array, base = places[i][2][q][part]
                            left[to + i * plan.row_blocks] = arrays[array][n + (base + shift)]
                    return carry

                for part, begin, end, shift in (
                    (0, 0, split, joint),
                    (1, split, blocks, joint - cut),
                ):
                    lax.fori_loop(
                        0,
                        lax.shift_right_logical(end - begin + RUN - 1, RUN_BITS),
                        functools.partial(run, part=part, begin=begin, end=end, shift=shift),
                        0,
                    )
                joint = joint + blocks

    hop = places[0][1]

    def finished(i):
        e = jnp.bitwise_xor(jnp.bitwise_and(grid_col, 7), 4 * hop + i)
        return pltpu.make_async_copy(
            result.at[i],
            out.at[:, pl.ds(pl.multiple_of(e * size, size), size), :],
            sems.at[i],
        )

    def one_group(i, carry):
        columns = [
            left[pl.ds(k * stride + i * plan.row_blocks, plan.row_blocks)].reshape(-1, BLOCK)
            for k in range(STEPS * plan.col_blocks)
        ]
        product = jnp.dot(
            jnp.concatenate(columns, axis=1), slabs[...], preferred_element_type=jnp.float32
        )
        result[i] = product.reshape(plan.row_blocks, size, width)
        finished(i).start()
        return carry

    lax.fori_loop(0, len(places), one_group, 0)
    for i in range(len(places)):
        finished(i).wait()


def part(plan, cut, lists, slabs, places, left, out):
    arrays = []

    def number(x):
        for i, array in enumerate(arrays):
            if array is x:
                return i
        arrays.append(x)
        return len(arrays) - 1

    places = [
        (flip, hop, [[(number(x), base) for x, base in both] for both in sources])
        for flip, hop, sources in places
    ]
    width = plan.tile_width
    shape = jax.ShapeDtypeStruct((plan.row_blocks, BLOCK, width), jnp.float32)
    extra = [left] if out is None else [left, out]
    count = 1 + len(arrays) + 1

    def body(*refs):
        part_kernel(plan, cut, places, *refs[:count], *refs[count + len(extra) :])

    return pl.pallas_call(
        body,
        out_shape=[shape, jax.ShapeDtypeStruct(left.shape, left.dtype)],
        in_specs=[ANY] + [VMEM] * (len(arrays) + 2) + [ANY] * (len(extra) - 1),
        out_specs=[ANY, VMEM],
        scratch_shapes=[
            pltpu.VMEM((len(places), plan.row_blocks, plan.piece, width), jnp.float32),
            pltpu.SMEM((STEPS, LIST), jnp.int32),
            pltpu.SemaphoreType.DMA((len(places),)),
            pltpu.SemaphoreType.DMA,
        ],
        input_output_aliases={count: 1} if out is None else {count: 1, count + 1: 0},
        cost_estimate=SMALL,
        compiler_params=pltpu.CompilerParams(vmem_limit_bytes=20 * 2**20),
        name="part",
    )(lists, *arrays, slabs, *extra)


def flipped(x, count, bits):
    return lax.ppermute(x, "row", [(i, i ^ bits) for i in range(count)])


def by_exchange(plan, lists, slabs, own, own_u):
    slabs = list(slabs)
    move = functools.partial(flipped, count=plan.row_count)
    tied = lambda *xs: lax.optimization_barrier(xs)
    u = own_u.shape[0]
    v = own.shape[0] - u
    slabs[1] = lax.ppermute(slabs[1], "col", [(0, 1), (1, 0)])
    far_u, near_u, own_x = move(own_u, bits=8), move(own_u, bits=4), move(own, bits=2)
    own_x, near_u, far_u, left, slabs[1] = tied(own_x, near_u, far_u, blank(plan), slabs[1])

    own_w = stacked((own, u, v), (own_x, u, v))
    far_w = move(own_w, bits=8)
    last_near = move(stacked((far_u, 0, u), (own_w, 0, 2 * v)), bits=4)
    near_far_x = move(stacked((near_u, 0, u), (far_u, 0, u)), bits=2)
    near_far_x, last_near, far_w = tied(near_far_x, last_near, far_w)

    last_xu = move(stacked((last_near, 0, u)), bits=2)
    last_w = move(far_w, bits=4)
    core = move(
        stacked(
            (own, 0, u + v),
            (own_x, 0, u + v),
            (far_u, 0, u),
            (near_u, 0, u),
            (last_near, 0, u + 2 * v),
            (near_far_x, 0, 2 * u),
            (far_w, 0, 2 * v),
        ),
        bits=1,
    )
    slabs = [slab.reshape(-1, plan.piece, plan.tile_width) for slab in slabs]
    right = stacked(*[(slab, 0, slab.shape[0]) for slab in slabs])
    right = right.reshape(STEPS * plan.tile_width, plan.tile_width)
    multiply = functools.partial(part, plan, u, lists, right)
    there = 2 * (u + v)
    out, left = multiply(
        [
            (0, 0, [[(own, 0), (own, u)], [(far_u, 0), (far_w, 0)]]),
            (1, 0, [[(core, 0), (core, u)], [(core, there), (core, there + 5 * u + 2 * v)]]),
            (2, 0, [[(own_x, 0), (own_x, u)], [(near_far_x, u), (far_w, v)]]),
            (
                3,
                0,
                [
                    [(core, u + v), (core, 2 * u + v)],
                    [(core, there + 4 * u + 2 * v), (core, there + 5 * u + 3 * v)],
                ],
            ),
        ],
        left,
        None,
    )
    last_xu, last_w, out = tied(last_xu, last_w, out)
    last_core = move(stacked((last_xu, 0, u), (last_w, 0, 2 * v)), bits=1)
    out, left = multiply(
        [
            (0, 1, [[(near_u, 0), (last_near, u)], [(last_near, 0), (last_w, 0)]]),
            (
                1,
                1,
                [
                    [(core, there + u), (core, there + 3 * u)],
                    [(core, there + 2 * u), (last_core, u)],
                ],
            ),
            (2, 1, [[(near_far_x, 0), (last_near, u + v)], [(last_xu, 0), (last_w, v)]]),
            (
                3,
                1,
                [
                    [(core, there + 3 * u + 2 * v), (core, there + 3 * u + v)],
                    [(last_core, 0), (last_core, u + v)],
                ],
            ),
        ],
        left,
        out,
    )
    return out.reshape(plan.tile_rows, plan.tile_width)


def multiply_kernel(plan, rows, mask, owner, lists, lefts, *refs):
    slabs = refs[: len(plan.shifts)]
    out, left, right, counts = refs[len(plan.shifts) :]
    grid_row = lax.axis_index("col")
    row0 = grid_row * plan.row_blocks
    width = plan.tile_width
    size = plan.piece

    @pl.when(pl.program_id(0) == 0)
    def _():
        for s, steps in enumerate(plan.shifts):
            for i, t in enumerate(steps):
                right[t * width : (t + 1) * width, :] = slabs[s][i * width : (i + 1) * width, :]
        for t in range(STEPS):
            counts[t] = sum(
                (lists[i, LIST - 1] for i in range(t % plan.col_count, t, plan.col_count)),
                jnp.int32(0),
            )

    def one_row(r, carry):
        block_row = row0 + pl.program_id(0) * rows + r
        for t in range(STEPS):
            root = owner[grid_row, t]
            group = lax.rem(grid_row + t, plan.col_count)
            for c in range(plan.col_blocks):
                kept = mask[block_row, root * plan.col_blocks + c]
                at = t * width + c * BLOCK

                @pl.when(kept == 1)
                def _():
                    have = counts[t]
                    for e in range(plan.group):
                        to = pl.multiple_of(r * BLOCK + e * size, size)
                        left[pl.ds(to, size), at : at + BLOCK] = lefts[
                            group * plan.group + e, have
                        ]
                    counts[t] = have + 1

                @pl.when(kept != 1)
                def _():
                    left[pl.ds(pl.multiple_of(r * BLOCK, BLOCK), BLOCK), at : at + BLOCK] = (
                        jnp.zeros((BLOCK, BLOCK), jnp.bfloat16)
                    )

        return carry

    lax.fori_loop(0, rows, one_row, 0)
    out[...] = jnp.dot(left[...], right[...], preferred_element_type=jnp.float32)


def multiply(plan, mask, owner, lists, lefts, slabs):
    rows = 4
    width = plan.tile_width
    return pl.pallas_call(
        functools.partial(multiply_kernel, plan, rows),
        grid=(plan.row_blocks // rows,),
        out_shape=jax.ShapeDtypeStruct((plan.tile_rows, width), jnp.float32),
        in_specs=[SMEM, SMEM, SMEM] + [VMEM] * (1 + len(slabs)),
        out_specs=pl.BlockSpec((rows * BLOCK, width), lambda i: (i, 0)),
        scratch_shapes=[
            pltpu.VMEM((rows * BLOCK, STEPS * width), jnp.bfloat16),
            pltpu.VMEM((STEPS * width, width), jnp.bfloat16),
            pltpu.SMEM((STEPS,), jnp.int32),
        ],
        compiler_params=pltpu.CompilerParams(vmem_limit_bytes=32 * 2**20),
        name="multiply",
    )(mask, owner, lists, lefts, *slabs)


def shards(density, block_mask, owner):
    row_count = lax.axis_size("row")
    col_count = lax.axis_size("col")
    plan = Plan(row_count, col_count, *density.shape)
    owner = owner.T
    most = plan.held * plan.cap
    most = plan.held * plan.cap
    if (row_count, col_count) == (16, 2):
        own, other = pack(plan, 2, block_mask, density)
        other = flipped(other, row_count, 1)
        small, middle = most * 5 // 16 * 2 + 2, most * 3 // 8 * 2
        sizes = [
            (small, plan.cap),
            (middle, plan.cap),
            (middle, middle),
            (most, plan.cap),
            (most, most),
        ]
        counts = counts_of(plan, sizes, block_mask, owner)

        def branch(capacity, chip_capacity):
            cut = capacity * 3 // 8 * 2

            def run(own, other, counts, owner, block_mask, density):
                chips = list(merge(plan, chip_capacity, counts, owner, own, other))
                for d in (3, 1, 2):
                    chips[d] = flipped(chips[d], row_count, 2 * d)
                slabs = slabs_of(plan, block_mask, owner, density)
                *slabs, block_mask = lax.optimization_barrier((*slabs, block_mask))
                lists = lists_of(plan, block_mask, owner)
                chips[3], *chips[:3], slabs, lists = lax.optimization_barrier(
                    (chips[3], *chips[:3], slabs, lists)
                )
                held = take(plan, [capacity, cut], counts, owner, chips)
                return by_exchange(plan, lists, slabs, *held)

            return run

        branches = [branch(*size) for size in sizes]
        return lax.switch(
            counts[STEPS], branches, own, other, counts, owner, block_mask, density
        )

    pieces = list(pack(plan, plan.group, block_mask, density))
    for k in range(1, plan.group):
        pieces[k] = flipped(pieces[k], row_count, k)
    lists = lists_of(plan, block_mask, owner)
    (held,) = pick(plan, [most], lists, owner, pieces)
    lefts = lax.all_gather(held, "row")
    slabs = [
        lax.ppermute(slab, "col", [(i, (i - s) % col_count) for i in range(col_count)])
        for s, slab in enumerate(slabs_of(plan, block_mask, owner, density))
    ]
    return multiply(plan, block_mask, owner, lists, lefts, slabs)


def solution(mesh):
    placed = (P("col", "row"), P(), P())
    return jax.shard_map(
        shards, mesh=mesh, in_specs=placed, out_specs=P("col", "row"), check_vma=False
    )
```

```python
import functools

import jax
import jax.numpy as jnp
from jax import lax
from jax.experimental import pallas as pl
from jax.experimental.pallas import tpu as pltpu
from jax.sharding import PartitionSpec as P

BLOCK = 128
STEPS = 4
GROUPS = 4
RUN_BITS = 2
RUN = 1 << RUN_BITS
LIST = 128

VMEM = pl.BlockSpec(memory_space=pltpu.VMEM)
SMEM = pl.BlockSpec(memory_space=pltpu.SMEM)
ANY = pl.BlockSpec(memory_space=pl.ANY)
SMALL = pl.CostEstimate(flops=1000, bytes_accessed=1000, transcendentals=0)
LARGE = pl.CostEstimate(flops=10**10, bytes_accessed=40 * 2**20, transcendentals=0)


class Plan:
    def __init__(self, row_count, col_count, tile_rows, tile_width):
        self.row_count = row_count
        self.col_count = col_count
        self.tile_rows = tile_rows
        self.tile_width = tile_width
        self.row_blocks = tile_rows // BLOCK
        self.col_blocks = tile_width // BLOCK
        self.cells = self.row_blocks * self.col_blocks
        self.group = row_count // col_count
        self.cap = self.cells * 3 // 5
        self.piece = BLOCK // self.group
        self.held = max(1, STEPS // col_count)
        self.shifts = [
            [t for t in range(STEPS) if t % col_count == s]
            for s in range(min(col_count, STEPS))
        ]


def list_blocks(plan, mask, row0, col0, put, marks):
    together = 4

    def some_rows(m, count):
        cells = [(m * together + i, c) for i in range(together) for c in range(plan.col_blocks)]
        kept = [mask[row0 + r, col0 + c] for r, c in cells]
        for (r, c), one in zip(cells, kept):
            put(count, r, c)
            count = count + one
        return count

    counts = [jnp.int32(0)]
    for first, last in zip(marks[:-1], marks[1:]):
        counts.append(
            lax.fori_loop(first // together, last // together, some_rows, counts[-1])
        )
    return counts


def pack_kernel(plan, mask_any, tile_any, *refs):
    *outs, tile, mask, listed, tile_sems, mask_sem = refs
    grid_col = lax.axis_index("row")
    row0 = lax.axis_index("col") * plan.row_blocks
    col0 = grid_col * plan.col_blocks
    chunks = 6
    chunk_blocks = plan.row_blocks // chunks
    marks = [q * chunk_blocks for q in range(chunks + 1)]

    mask_copy = pltpu.make_async_copy(mask_any, mask, mask_sem)
    mask_copy.start()
    copies = []
    for q in range(chunks):
        rows = pl.ds(marks[q] * plan.group, chunk_blocks * plan.group)
        copy = pltpu.make_async_copy(tile_any.at[rows], tile.at[rows], tile_sems.at[q])
        copy.start()
        copies.append(copy)
    mask_copy.wait()

    def put(n, r, c):
        listed[n] = 4 * r + c

    counts = list_blocks(plan, mask, row0, col0, put, marks)
    place = lax.rem(grid_col, plan.group)
    parts = [jnp.bitwise_xor(place, k) for k in range(plan.group)]

    def one_block(n, carry):
        code = listed[n]
        top = lax.shift_right_logical(code, 2) * plan.group
        left = pl.multiple_of(jnp.bitwise_and(code, 3) * BLOCK, BLOCK)
        for k in range(plan.group):
            block = tile[top + parts[k], :, pl.ds(left, BLOCK)]
            outs[k % len(outs)][k // len(outs), n] = block
        return carry

    for q in range(chunks):
        copies[q].wait()
        lax.fori_loop(counts[q], counts[q + 1], one_block, 0)


def pack(plan, count, mask, tile):
    pieces = (plan.group // count, plan.cap, plan.piece, BLOCK)
    tile = tile.reshape(-1, plan.piece, plan.tile_width)
    return pl.pallas_call(
        functools.partial(pack_kernel, plan),
        out_shape=[jax.ShapeDtypeStruct(pieces, jnp.bfloat16)] * count,
        in_specs=[ANY, ANY],
        out_specs=[VMEM] * count,
        scratch_shapes=[
            pltpu.VMEM(tile.shape, jnp.bfloat16),
            pltpu.SMEM(mask.shape, jnp.int32),
            pltpu.SMEM((plan.cells,), jnp.int32),
            pltpu.SemaphoreType.DMA((6,)),
            pltpu.SemaphoreType.DMA,
        ],
        compiler_params=pltpu.CompilerParams(vmem_limit_bytes=60 * 2**20),
        name="pack",
    )(mask, tile)


def slabs_kernel(plan, mask, owner, tile, *refs):
    slabs = refs[: len(plan.shifts)]
    found, sems = refs[len(plan.shifts) :]
    grid_row = lax.axis_index("col")
    row0 = grid_row * plan.row_blocks
    col0 = lax.axis_index("row") * plan.col_blocks
    width = plan.tile_width
    wanted = []
    for s, steps in enumerate(plan.shifts):
        target = lax.rem(grid_row - s + plan.col_count, plan.col_count)
        for i, t in enumerate(steps):
            first = lax.rem(owner[target, t], plan.group)
            copy = pltpu.make_async_copy(
                tile.at[pl.ds(pl.multiple_of(first * width, width), width)],
                found.at[t],
                sems.at[t],
            )
            copy.start()
            wanted.append((s, i, t, first * plan.col_blocks, copy))
    for s, i, t, first, copy in wanted:
        copy.wait()
        for r in range(plan.col_blocks):
            for c in range(plan.col_blocks):
                kept = mask[row0 + first + r, col0 + c]
                block = found[t, r * BLOCK : (r + 1) * BLOCK, c * BLOCK : (c + 1) * BLOCK]
                to = i * width + r * BLOCK
                slabs[s][to : to + BLOCK, c * BLOCK : (c + 1) * BLOCK] = jnp.where(
                    kept == 1, block, jnp.zeros_like(block)
                )


def slabs_of(plan, mask, owner, tile):
    width = plan.tile_width
    return pl.pallas_call(
        functools.partial(slabs_kernel, plan),
        out_shape=[
            jax.ShapeDtypeStruct((len(s) * width, width), jnp.bfloat16) for s in plan.shifts
        ],
        in_specs=[SMEM, SMEM, ANY],
        out_specs=[VMEM] * len(plan.shifts),
        scratch_shapes=[
            pltpu.VMEM((STEPS, width, width), jnp.bfloat16),
            pltpu.SemaphoreType.DMA((STEPS,)),
        ],
        cost_estimate=SMALL,
        compiler_params=pltpu.CompilerParams(vmem_limit_bytes=8 * 2**20),
        name="slabs",
    )(mask, owner, tile)


def lists_kernel(plan, mask, owner, lists):
    grid_row = lax.axis_index("col")
    row0 = grid_row * plan.row_blocks
    for t in range(STEPS):

        def put(n, r, c):
            lists[t, n] = c * GROUPS * plan.row_blocks + r

        col0 = owner[grid_row, t] * plan.col_blocks
        count = list_blocks(plan, mask, row0, col0, put, [0, plan.row_blocks])[-1]
        lists[t, LIST - 1] = count


def lists_of(plan, mask, owner):
    return pl.pallas_call(
        functools.partial(lists_kernel, plan),
        out_shape=jax.ShapeDtypeStruct((STEPS, LIST), jnp.int32),
        in_specs=[SMEM, SMEM],
        out_specs=SMEM,
        cost_estimate=SMALL,
        compiler_params=pltpu.CompilerParams(vmem_limit_bytes=2 * 2**20),
        name="lists",
    )(mask, owner)


def counts_kernel(plan, branches, mask, owner, counts):
    grid_row = lax.axis_index("col")
    most = jnp.int32(0)
    chip_most = jnp.int32(0)
    for g in range(plan.col_count):
        kept = mask[g * plan.row_blocks : (g + 1) * plan.row_blocks, :]
        column = lax.broadcasted_iota(jnp.int32, kept.shape, 1)
        found = []
        for t in range(STEPS):
            col0 = owner[g, t] * plan.col_blocks
            inside = (column >= col0) & (column < col0 + plan.col_blocks)
            found.append(jnp.sum(jnp.where(inside, kept, 0)))

        @pl.when(grid_row == g)
        def _():
            for t in range(STEPS):
                counts[t] = found[t]

        for t in range(STEPS // 2):
            total = found[t] + found[t + 2]
            one_chip = jnp.bitwise_xor(owner[g, t], owner[g, t + 2]) == 1
            most = jnp.maximum(most, total)
            chip_most = jnp.maximum(chip_most, jnp.where(one_chip, total, 0))
    choice = jnp.int32(len(branches) - 1)
    for i, (capacity, chip_capacity) in reversed(list(enumerate(branches))):
        choice = jnp.where((most <= capacity) & (chip_most <= chip_capacity), i, choice)
    counts[STEPS] = choice


def counts_of(plan, branches, mask, owner):
    return pl.pallas_call(
        functools.partial(counts_kernel, plan, branches),
        out_shape=jax.ShapeDtypeStruct((STEPS + 1,), jnp.int32),
        in_specs=[VMEM, SMEM],
        out_specs=SMEM,
        cost_estimate=SMALL,
        compiler_params=pltpu.CompilerParams(vmem_limit_bytes=2 * 2**20),
        name="counts",
    )(mask, owner)


def copy_blocks(count, copy):
    def run(m, carry):
        for n in range(RUN):
            copy(jnp.minimum(m * RUN + n, count - 1))
        return carry

    lax.fori_loop(0, lax.shift_right_logical(count + RUN - 1, RUN_BITS), run, 0)


def used_tiles(plan, counts, owner):
    grid_row = lax.axis_index("col")
    grid_col = lax.axis_index("row")
    first = lax.rem(lax.div(grid_col, plan.group) + grid_row, 2)
    roots = [lax.rem(owner[grid_row, first + 2 * i], plan.group) for i in range(2)]
    blocks = [counts[first + 2 * i] for i in range(2)]
    return lax.rem(grid_col, plan.group), roots, blocks


def merge_kernel(plan, counts, owner, own, other, *refs):
    *outs, joint = refs
    place, roots, blocks = used_tiles(plan, counts, owner)
    core = jnp.bitwise_and(place, 1)
    lower = place - core
    at = jnp.int32(0)
    for i in range(2):
        count = jnp.where(
            roots[0] == lower + i, blocks[0], jnp.where(roots[1] == lower + i, blocks[1], 0)
        )
        for source, mine in ((own, core == i), (other, core != i)):

            def copy(n, source=source, at=at):
                for d in range(len(outs)):
                    joint[d, at + n] = source[d, n]

            copy_blocks(jnp.where(mine, count, 0), copy)
        at = at + count

    def some(n, carry):
        for d, out in enumerate(outs):
            out[n] = joint[d, n]
        return carry

    lax.fori_loop(0, outs[0].shape[0], some, 0)


def merge(plan, capacity, counts, owner, own, other):
    count = plan.group // 2
    shape = jax.ShapeDtypeStruct((capacity, plan.piece, BLOCK), jnp.bfloat16)
    return pl.pallas_call(
        functools.partial(merge_kernel, plan),
        out_shape=[shape] * count,
        in_specs=[SMEM, SMEM, VMEM, VMEM],
        out_specs=[VMEM] * count,
        scratch_shapes=[pltpu.VMEM((count, 2 * plan.cap, plan.piece, BLOCK), jnp.bfloat16)],
        compiler_params=pltpu.CompilerParams(vmem_limit_bytes=10 * 2**20),
        name="merge",
    )(counts, owner, own, other)


def take_kernel(plan, counts, owner, *refs):
    chips, outs, joint = refs[:-3], refs[-3:-1], refs[-1]
    place, roots, blocks = used_tiles(plan, counts, owner)
    at = jnp.int32(0)
    for i in range(2):
        root, other = roots[i], roots[1 - i]
        behind = (jnp.bitwise_and(root, 1) == 1) & (other == root - 1)
        start = jnp.where(behind, blocks[1 - i], 0)
        distance = lax.shift_right_logical(jnp.bitwise_xor(root, place), 1)
        for d, chip in enumerate(chips):

            def copy(n, chip=chip, at=at):
                joint[at + n] = chip[start + n]

            copy_blocks(jnp.where(distance == d, blocks[i], 0), copy)
        at = at + blocks[i]
    low = 0
    for out in outs:

        def some(m, carry, low=low, out=out):
            out[pl.ds(2 * m, 2)] = joint[pl.ds(low + 2 * m, 2)]
            return carry

        lax.fori_loop(0, out.shape[0] // 2, some, 0)
        low += out.shape[0]


def take(plan, sizes, counts, owner, chips):
    return pl.pallas_call(
        functools.partial(take_kernel, plan),
        out_shape=[
            jax.ShapeDtypeStruct((size, plan.piece, BLOCK), jnp.bfloat16) for size in sizes
        ],
        in_specs=[SMEM, SMEM] + [VMEM] * len(chips),
        out_specs=[VMEM] * len(sizes),
        scratch_shapes=[pltpu.VMEM((2 * plan.cap, plan.piece, BLOCK), jnp.bfloat16)],
        compiler_params=pltpu.CompilerParams(vmem_limit_bytes=8 * 2**20),
        name="take",
    )(counts, owner, *chips)


def pick_kernel(plan, lists, owner, *refs):
    pieces = refs[: plan.group]
    joint = refs[-1]
    outs = refs[plan.group : -1]
    grid_row = lax.axis_index("col")
    grid_col = lax.axis_index("row")
    mine = lax.div(grid_col, plan.group)
    place = lax.rem(grid_col, plan.group)
    first = lax.rem(mine - grid_row + plan.col_count, plan.col_count)
    at = jnp.int32(0)
    for i in range(plan.held):
        step = lax.rem(first + i * plan.col_count, STEPS)
        root = lax.rem(owner[grid_row, step], plan.group)
        for k, piece in enumerate(pieces):

            @pl.when(root == jnp.bitwise_xor(place, k))
            def _():
                joint[pl.ds(at, plan.cap)] = piece[0]

        at = at + lists[step, LIST - 1]
    low = 0
    for out in outs:
        out[...] = joint[low : low + out.shape[0]]
        low += out.shape[0]


def pick(plan, sizes, lists, owner, pieces):
    return pl.pallas_call(
        functools.partial(pick_kernel, plan),
        out_shape=[
            jax.ShapeDtypeStruct((size, plan.piece, BLOCK), jnp.bfloat16) for size in sizes
        ],
        in_specs=[SMEM, SMEM] + [VMEM] * plan.group,
        out_specs=[VMEM] * len(sizes),
        scratch_shapes=[
            pltpu.VMEM((plan.held * plan.cap, plan.piece, BLOCK), jnp.bfloat16),
        ],
        compiler_params=pltpu.CompilerParams(vmem_limit_bytes=8 * 2**20),
        name="pick",
    )(lists, owner, *pieces)


def stack_kernel(ranges, *refs):
    to = 0
    for ref, (low, count) in zip(refs, ranges):
        together = next(n for n in (8, 6, 4, 2, 1) if count % n == 0)

        def some(m, carry, ref=ref, low=low, to=to, together=together):
            refs[-1][pl.ds(to + m * together, together)] = ref[
                pl.ds(low + m * together, together)
            ]
            return carry

        lax.fori_loop(0, count // together, some, 0)
        to += count


def stacked(*pieces):
    ranges = [(low, count) for _, low, count in pieces]
    rows = sum(count for _, count in ranges)
    first = pieces[0][0]
    return pl.pallas_call(
        functools.partial(stack_kernel, ranges),
        out_shape=jax.ShapeDtypeStruct((rows,) + first.shape[1:], first.dtype),
        in_specs=[VMEM] * len(pieces),
        out_specs=VMEM,
        cost_estimate=SMALL,
        compiler_params=pltpu.CompilerParams(vmem_limit_bytes=6 * 2**20),
        name="stacked",
    )(*[array for array, _, _ in pieces])


def blank(plan):
    together = 2 * plan.row_blocks

    def body(out):
        def some(m, carry):
            out[pl.ds(m * together, together)] = jnp.zeros((together,) + out.shape[1:], out.dtype)
            return carry

        lax.fori_loop(0, out.shape[0] // together, some, 0)

    parts = STEPS * plan.col_blocks * GROUPS * plan.row_blocks
    return pl.pallas_call(
        body,
        out_shape=jax.ShapeDtypeStruct((parts, plan.piece, BLOCK), jnp.bfloat16),
        out_specs=VMEM,
        cost_estimate=SMALL,
        compiler_params=pltpu.CompilerParams(vmem_limit_bytes=8 * 2**20),
        name="blank",
    )()


def part_kernel(plan, cut, places, lists_any, *refs):
    count = 1 + max(array for _, _, sources in places for both in sources for array, _ in both)
    arrays = refs[:count]
    slabs = refs[count]
    out, left, result, lists, sems, lists_sem = refs[-6:]
    grid_row = lax.axis_index("col")
    grid_col = lax.axis_index("row")
    width = plan.tile_width
    size = plan.piece
    stride = GROUPS * plan.row_blocks
    lists_copy = pltpu.make_async_copy(lists_any, lists, lists_sem)
    lists_copy.start()
    lists_copy.wait()
    for hop in sorted({place[1] for place in places}):
        chosen = range(len(places))
        level = jnp.bitwise_xor(lax.shift_right_logical(grid_col, 2), hop)
        for q in range(2):
            half = lax.shift_right_logical(jnp.bitwise_xor(level, 2 * q), 1)
            first = jnp.bitwise_xor(half, grid_row)
            joint = jnp.int32(0)
            for s in range(plan.held):
                step = first + 2 * s
                origin = (first * plan.held + s) * plan.col_blocks * stride
                blocks = lists[step, LIST - 1]
                split = jnp.minimum(blocks, jnp.maximum(cut - joint, 0))

                def run(m, carry, part, begin, end, shift):
                    for n in range(RUN):
                        n = jnp.minimum(begin + m * RUN + n, end - 1)
                        to = origin + lists[step, n]
                        for i in chosen:
                            array, base = places[i][2][q][part]
                            left[to + i * plan.row_blocks] = arrays[array][n + (base + shift)]
                    return carry

                for part, begin, end, shift in (
                    (0, 0, split, joint),
                    (1, split, blocks, joint - cut),
                ):
                    lax.fori_loop(
                        0,
                        lax.shift_right_logical(end - begin + RUN - 1, RUN_BITS),
                        functools.partial(run, part=part, begin=begin, end=end, shift=shift),
                        0,
                    )
                joint = joint + blocks

    hop = places[0][1]

    def finished(i):
        e = jnp.bitwise_xor(jnp.bitwise_and(grid_col, 7), 4 * hop + i)
        return pltpu.make_async_copy(
            result.at[i],
            out.at[:, pl.ds(pl.multiple_of(e * size, size), size), :],
            sems.at[i],
        )

    def one_group(i, carry):
        columns = [
            left[pl.ds(k * stride + i * plan.row_blocks, plan.row_blocks)].reshape(-1, BLOCK)
            for k in range(STEPS * plan.col_blocks)
        ]
        product = jnp.dot(
            jnp.concatenate(columns, axis=1), slabs[...], preferred_element_type=jnp.float32
        )
        result[i] = product.reshape(plan.row_blocks, size, width)
        finished(i).start()
        return carry

    lax.fori_loop(0, len(places), one_group, 0)
    for i in range(len(places)):
        finished(i).wait()


def part(plan, cut, lists, slabs, places, left, out):
    arrays = []

    def number(x):
        for i, array in enumerate(arrays):
            if array is x:
                return i
        arrays.append(x)
        return len(arrays) - 1

    places = [
        (flip, hop, [[(number(x), base) for x, base in both] for both in sources])
        for flip, hop, sources in places
    ]
    width = plan.tile_width
    shape = jax.ShapeDtypeStruct((plan.row_blocks, BLOCK, width), jnp.float32)
    extra = [left] if out is None else [left, out]
    count = 1 + len(arrays) + 1

    def body(*refs):
        part_kernel(plan, cut, places, *refs[:count], *refs[count + len(extra) :])

    return pl.pallas_call(
        body,
        out_shape=[shape, jax.ShapeDtypeStruct(left.shape, left.dtype)],
        in_specs=[ANY] + [VMEM] * (len(arrays) + 2) + [ANY] * (len(extra) - 1),
        out_specs=[ANY, VMEM],
        scratch_shapes=[
            pltpu.VMEM((len(places), plan.row_blocks, plan.piece, width), jnp.float32),
            pltpu.SMEM((STEPS, LIST), jnp.int32),
            pltpu.SemaphoreType.DMA((len(places),)),
            pltpu.SemaphoreType.DMA,
        ],
        input_output_aliases={count: 1} if out is None else {count: 1, count + 1: 0},
        cost_estimate=SMALL,
        compiler_params=pltpu.CompilerParams(vmem_limit_bytes=20 * 2**20),
        name="part",
    )(lists, *arrays, slabs, *extra)


def flipped(x, count, bits):
    return lax.ppermute(x, "row", [(i, i ^ bits) for i in range(count)])


def by_exchange(plan, lists, slabs, own_u, own_v):
    slabs = list(slabs)
    move = functools.partial(flipped, count=plan.row_count)
    tied = lambda *xs: lax.optimization_barrier(xs)
    u, v = own_u.shape[0], own_v.shape[0]
    slabs[1] = lax.ppermute(slabs[1], "col", [(0, 1), (1, 0)])
    far_u, near_u = move(own_u, bits=8), move(own_u, bits=4)
    own_xv, own_xu = move(own_v, bits=2), move(own_u, bits=2)
    own_xv, own_xu, near_u, far_u, left, slabs[1] = tied(
        own_xv, own_xu, near_u, far_u, blank(plan), slabs[1]
    )

    own_w = stacked((own_v, 0, v), (own_xv, 0, v))
    far_w = move(own_w, bits=8)
    last_near = move(stacked((far_u, 0, u), (own_w, 0, 2 * v)), bits=4)
    near_far_x = move(stacked((near_u, 0, u), (far_u, 0, u)), bits=2)
    near_far_x, last_near, far_w = tied(near_far_x, last_near, far_w)

    last_xu = move(stacked((last_near, 0, u)), bits=2)
    last_w = move(far_w, bits=4)
    core = move(
        stacked(
            (own_u, 0, u),
            (own_v, 0, v),
            (own_xu, 0, u),
            (own_xv, 0, v),
            (far_u, 0, u),
            (near_u, 0, u),
            (last_near, 0, u + 2 * v),
            (near_far_x, 0, 2 * u),
            (far_w, 0, 2 * v),
        ),
        bits=1,
    )
    slabs = [slab.reshape(-1, plan.piece, plan.tile_width) for slab in slabs]
    right = stacked(*[(slab, 0, slab.shape[0]) for slab in slabs])
    right = right.reshape(STEPS * plan.tile_width, plan.tile_width)
    multiply = functools.partial(part, plan, u, lists, right)
    there = 2 * (u + v)
    out, left = multiply(
        [
            (0, 0, [[(own_u, 0), (own_v, 0)], [(far_u, 0), (far_w, 0)]]),
            (1, 0, [[(core, 0), (core, u)], [(core, there), (core, there + 5 * u + 2 * v)]]),
            (2, 0, [[(own_xu, 0), (own_xv, 0)], [(near_far_x, u), (far_w, v)]]),
            (
                3,
                0,
                [
                    [(core, u + v), (core, 2 * u + v)],
                    [(core, there + 4 * u + 2 * v), (core, there + 5 * u + 3 * v)],
                ],
            ),
        ],
        left,
        None,
    )
    last_xu, last_w, out = tied(last_xu, last_w, out)
    last_core = move(stacked((last_xu, 0, u), (last_w, 0, 2 * v)), bits=1)
    out, left = multiply(
        [
            (0, 1, [[(near_u, 0), (last_near, u)], [(last_near, 0), (last_w, 0)]]),
            (
                1,
                1,
                [
                    [(core, there + u), (core, there + 3 * u)],
                    [(core, there + 2 * u), (last_core, u)],
                ],
            ),
            (2, 1, [[(near_far_x, 0), (last_near, u + v)], [(last_xu, 0), (last_w, v)]]),
            (
                3,
                1,
                [
                    [(core, there + 3 * u + 2 * v), (core, there + 3 * u + v)],
                    [(last_core, 0), (last_core, u + v)],
                ],
            ),
        ],
        left,
        out,
    )
    return out.reshape(plan.tile_rows, plan.tile_width)


def multiply_kernel(plan, rows, mask, owner, lists, lefts, *refs):
    slabs = refs[: len(plan.shifts)]
    out, left, right, counts = refs[len(plan.shifts) :]
    grid_row = lax.axis_index("col")
    row0 = grid_row * plan.row_blocks
    width = plan.tile_width
    size = plan.piece

    @pl.when(pl.program_id(0) == 0)
    def _():
        for s, steps in enumerate(plan.shifts):
            for i, t in enumerate(steps):
                right[t * width : (t + 1) * width, :] = slabs[s][i * width : (i + 1) * width, :]
        for t in range(STEPS):
            counts[t] = sum(
                (lists[i, LIST - 1] for i in range(t % plan.col_count, t, plan.col_count)),
                jnp.int32(0),
            )

    def one_row(r, carry):
        block_row = row0 + pl.program_id(0) * rows + r
        for t in range(STEPS):
            root = owner[grid_row, t]
            group = lax.rem(grid_row + t, plan.col_count)
            for c in range(plan.col_blocks):
                kept = mask[block_row, root * plan.col_blocks + c]
                at = t * width + c * BLOCK

                @pl.when(kept == 1)
                def _():
                    have = counts[t]
                    for e in range(plan.group):
                        to = pl.multiple_of(r * BLOCK + e * size, size)
                        left[pl.ds(to, size), at : at + BLOCK] = lefts[
                            group * plan.group + e, have
                        ]
                    counts[t] = have + 1

                @pl.when(kept != 1)
                def _():
                    left[pl.ds(pl.multiple_of(r * BLOCK, BLOCK), BLOCK), at : at + BLOCK] = (
                        jnp.zeros((BLOCK, BLOCK), jnp.bfloat16)
                    )

        return carry

    lax.fori_loop(0, rows, one_row, 0)
    out[...] = jnp.dot(left[...], right[...], preferred_element_type=jnp.float32)


def multiply(plan, mask, owner, lists, lefts, slabs):
    rows = 4
    width = plan.tile_width
    return pl.pallas_call(
        functools.partial(multiply_kernel, plan, rows),
        grid=(plan.row_blocks // rows,),
        out_shape=jax.ShapeDtypeStruct((plan.tile_rows, width), jnp.float32),
        in_specs=[SMEM, SMEM, SMEM] + [VMEM] * (1 + len(slabs)),
        out_specs=pl.BlockSpec((rows * BLOCK, width), lambda i: (i, 0)),
        scratch_shapes=[
            pltpu.VMEM((rows * BLOCK, STEPS * width), jnp.bfloat16),
            pltpu.VMEM((STEPS * width, width), jnp.bfloat16),
            pltpu.SMEM((STEPS,), jnp.int32),
        ],
        compiler_params=pltpu.CompilerParams(vmem_limit_bytes=32 * 2**20),
        name="multiply",
    )(mask, owner, lists, lefts, *slabs)


def shards(density, block_mask, owner):
    row_count = lax.axis_size("row")
    col_count = lax.axis_size("col")
    plan = Plan(row_count, col_count, *density.shape)
    owner = owner.T
    most = plan.held * plan.cap
    most = plan.held * plan.cap
    if (row_count, col_count) == (16, 2):
        own, other = pack(plan, 2, block_mask, density)
        other = flipped(other, row_count, 1)
        small, middle = most * 5 // 16 * 2 + 2, most * 3 // 8 * 2
        sizes = [
            (small, plan.cap),
            (middle, plan.cap),
            (middle, middle),
            (most, plan.cap),
            (most, most),
        ]
        counts = counts_of(plan, sizes, block_mask, owner)

        def branch(capacity, chip_capacity):
            cut = capacity * 3 // 8 * 2

            def run(own, other, counts, owner, block_mask, density):
                chips = list(merge(plan, chip_capacity, counts, owner, own, other))
                for d in (3, 1, 2):
                    chips[d] = flipped(chips[d], row_count, 2 * d)
                slabs = slabs_of(plan, block_mask, owner, density)
                *slabs, block_mask = lax.optimization_barrier((*slabs, block_mask))
                lists = lists_of(plan, block_mask, owner)
                chips[3], *chips[:3], slabs, lists = lax.optimization_barrier(
                    (chips[3], *chips[:3], slabs, lists)
                )
                held = take(plan, [cut, capacity - cut], counts, owner, chips)
                return by_exchange(plan, lists, slabs, *held)

            return run

        branches = [branch(*size) for size in sizes]
        return lax.switch(
            counts[STEPS], branches, own, other, counts, owner, block_mask, density
        )

    pieces = list(pack(plan, plan.group, block_mask, density))
    for k in range(1, plan.group):
        pieces[k] = flipped(pieces[k], row_count, k)
    lists = lists_of(plan, block_mask, owner)
    (held,) = pick(plan, [most], lists, owner, pieces)
    lefts = lax.all_gather(held, "row")
    slabs = [
        lax.ppermute(slab, "col", [(i, (i - s) % col_count) for i in range(col_count)])
        for s, slab in enumerate(slabs_of(plan, block_mask, owner, density))
    ]
    return multiply(plan, block_mask, owner, lists, lefts, slabs)


def solution(mesh):
    placed = (P("col", "row"), P(), P())
    return jax.shard_map(
        shards, mesh=mesh, in_specs=placed, out_specs=P("col", "row"), check_vma=False
    )
```
